1024 devices in a mesh: node: 64 (over y, x, core), local: 16 (over z).
Axes of the slice: x: 4, y: 8, z: 16, core: 2. Of those that a mesh axis runs over, the one named last changes fastest.
Arguments:
- output_gradient: bfloat16 [8192, 3584], P(('node', 'local')), may hold values from -6 to 6
- expert_ids: int32 [8192, 8], P(('node', 'local')), may hold values from 0 to 127, as said below
- gate_weights: bfloat16 [8192, 8], P(('node', 'local')), may hold values from 0.099609375 to 0.59765625
- saved_gate: bfloat16 [524288, 128], P(('node', 'local')), may hold values from -6 to 6
- saved_up: bfloat16 [524288, 128], P(('node', 'local')), may hold values from -6 to 6
- w_gate: bfloat16 [1024, 3584, 128], P(('node', 'local')), may hold values from -0.375 to 0.375
- w_up: bfloat16 [1024, 3584, 128], P(('node', 'local')), may hold values from -0.375 to 0.375
- w_down: bfloat16 [1024, 128, 3584], P(('node', 'local')), may hold values from -0.0234375 to 0.0234375
Outputs:
- grad_in: bfloat16 [8192, 3584], P(('node', 'local'))
- grad_gate: bfloat16 [8192, 8], P(('node', 'local'))
The draws below stay inside these ranges and needn't reach their ends.
Inputs may be any that keep to these rules, and one draw needn't show every extreme that they name: `expert_ids`: each token names 8 different experts, columns 2j and 2j+1 two experts of one node group (expert E lies in group E // 2), and its 4 groups differ. At most 1 token of one device name a given node group, and some group is named that often by every device. Over the tokens of all devices with one local index, at most 32 name a given expert, and in every draw some expert of some node group reaches that from every local index.
All inputs are finite; a program needn't handle non-finite values.
Results may differ from the reference program's by a relative error of at most 0.015.
Values may be sent and summed in bfloat16 or wider, within the bound.
No kernel may reach another device: no remote copies, remote signals or barrier semaphores. Data moves between devices by JAX's collectives and lax.ppermute only.
A program may use at most 32 MiB of HBM per device.

```python
import jax
import jax.numpy as jnp
from jax import lax

D = 3584
FFE = 1024
EXP_NODE = 2
TOPK = 8
NODES_TOK = 4
TOK_DEV = 8
SHARDS = 8
HIDDEN_PER_SHARD = 128
CAP = 1
SLOTS = 32
ROWS = 512
EXPERTS = 128
TOKENS = 8192
N_NODE = 64
N_LOCAL = 16


def draw_expert_ids(key, part):
    key = jax.random.fold_in(key, 11)
    keys = jax.random.split(key, 7)
    perms = jax.vmap(lambda sub: jax.random.permutation(sub, N_NODE))(jax.random.split(keys[0], N_LOCAL))
    hottest = jax.random.randint(keys[1], (N_NODE,), 0, EXP_NODE)
    filled = jax.random.randint(keys[2], (N_NODE,), 0, 2)
    forced = jax.random.randint(keys[6], (), 0, N_NODE)
    filled = jnp.maximum(filled, (jnp.arange(N_NODE, dtype=jnp.int32) == forced).astype(jnp.int32))
    token = jnp.arange(TOKENS, dtype=jnp.int32)
    device_index = token // TOK_DEV
    src_node = device_index // N_LOCAL
    src_local = device_index % N_LOCAL
    within = token % TOK_DEV
    order = within[:, None] * NODES_TOK + jnp.arange(NODES_TOK, dtype=jnp.int32)[None, :]
    offset = perms[src_local[:, None], order % N_NODE].astype(jnp.int32)
    node = (src_node[:, None] + offset) % N_NODE
    flip = jnp.maximum(jax.random.randint(keys[3], (TOKENS, NODES_TOK), 0, 2), filled[node])
    other = jax.random.randint(keys[4], (TOKENS, NODES_TOK), 1, EXP_NODE)
    skip = jax.random.randint(keys[5], (TOKENS, NODES_TOK), 1, EXP_NODE)
    hot = hottest[node]
    first = jnp.where(flip > 0, hot, (hot + skip % 3 + 1) % EXP_NODE)
    second = jnp.where(flip > 0, (hot + other) % EXP_NODE, (hot + (skip + 1) % 3 + 1) % EXP_NODE)
    ids = jnp.stack([node * EXP_NODE + first, node * EXP_NODE + second], axis=2)
    return ids.reshape(TOKENS, TOPK).astype(jnp.int32)


def block_levels(stream_key, dims, shards, low, high):
    factor_of = 1.0
    for dim, parts in shards:
        steps = jax.random.uniform(jax.random.fold_in(jax.random.fold_in(stream_key, 6), dim), (parts,), jnp.float32, low / len(shards), high / len(shards))
        factor_of = factor_of * jnp.repeat(jnp.exp(steps), dims[dim] // parts).reshape((-1,) + (1,) * (len(dims) - 1 - dim))
    return factor_of


def centred(rng, extent, deviation, reach, cuts=(), held_as=jnp.bfloat16):
    array = deviation * jax.random.normal(rng, extent, jnp.float32)
    if cuts:
        array = array * block_levels(rng, extent, cuts, -0.22, 0.18)
    return jnp.clip(array, -reach, reach).astype(held_as)


def setup_inputs(seed: int = 0) -> dict:
    seeds = jax.random.split(jax.random.key(seed), 9)
    return {
        "output_gradient": centred(seeds[0], (TOKENS, D), 1.0, 6.0, ((0, 1024),)),
        "expert_ids": draw_expert_ids(jax.random.fold_in(seeds[8], 71), 0),
        "gate_weights": jnp.clip(0.099609375 + 0.49804688 * jax.random.uniform(seeds[2], (TOKENS, TOPK), jnp.float32) ** block_levels(seeds[2], (TOKENS, TOPK), ((0, 1024),), -0.2, 0.2), 0.099609375, 0.59765625).astype(jnp.bfloat16),
        "saved_gate": centred(seeds[3], (N_NODE * N_LOCAL * ROWS, HIDDEN_PER_SHARD), 1.0, 6.0, ((0, 1024),)),
        "saved_up": centred(seeds[4], (N_NODE * N_LOCAL * ROWS, HIDDEN_PER_SHARD), 1.0, 6.0, ((0, 1024),)),
        "w_gate": centred(seeds[5], (N_NODE * N_LOCAL, D, HIDDEN_PER_SHARD), (FFE // 4) ** -0.5, 0.375, ((0, 1024),)),
        "w_up": centred(seeds[6], (N_NODE * N_LOCAL, D, HIDDEN_PER_SHARD), (FFE // 4) ** -0.5, 0.375, ((0, 1024),)),
        "w_down": centred(seeds[7], (N_NODE * N_LOCAL, HIDDEN_PER_SHARD, D), (16 * D) ** -0.5, 0.0234375, ((0, 1024),)),
    }


def route_rows(expert_ids):
    tokens = expert_ids.shape[0]
    pairs = expert_ids.reshape(tokens, NODES_TOK, 2)
    dest_node = pairs[:, :, 0] // EXP_NODE
    local_exp = pairs % EXP_NODE
    token = jnp.arange(tokens, dtype=jnp.int32)
    device_index = token // TOK_DEV
    src_node = device_index // N_LOCAL
    src_local = device_index % N_LOCAL
    per_device = dest_node.reshape(N_NODE * N_LOCAL, TOK_DEV * NODES_TOK)
    node_hit = (per_device[:, :, None] == jnp.arange(N_NODE, dtype=jnp.int32)[None, None, :]).astype(jnp.int32)
    earlier = jnp.cumsum(node_hit, axis=1) - node_hit
    slot = jnp.sum(earlier * node_hit, axis=2).reshape(tokens, NODES_TOK)
    receive = src_node[:, None] * CAP + slot
    receiver = dest_node * N_LOCAL + src_local[:, None]
    flat = receiver * (N_NODE * CAP) + receive
    expert_hit = (local_exp[:, :, :, None] == jnp.arange(EXP_NODE, dtype=jnp.int32)[None, None, None, :]).astype(jnp.int32)
    marks = jnp.zeros((N_NODE * N_LOCAL * N_NODE * CAP, EXP_NODE), jnp.int32)
    marks = marks.at[flat.reshape(-1)].add(jnp.sum(expert_hit, axis=2).reshape(-1, EXP_NODE))
    marks = marks.reshape(N_NODE * N_LOCAL, N_NODE * CAP, EXP_NODE)
    ahead = (jnp.cumsum(marks, axis=1) - marks).reshape(-1, EXP_NODE)
    position = ahead[flat[:, :, None], local_exp]
    expert = dest_node[:, :, None] * EXP_NODE + local_exp
    row = expert * ROWS + src_local[:, None, None] * SLOTS + position
    return row.reshape(-1).astype(jnp.int32)


def reference(output_gradient, expert_ids, gate_weights, saved_gate, saved_up, w_gate, w_up, w_down):
    tokens = output_gradient.shape[0]
    rows = route_rows(expert_ids)
    route = jnp.arange(tokens * TOPK, dtype=jnp.int32)
    holder = jnp.full((EXPERTS * ROWS,), tokens * TOPK, jnp.int32).at[rows].set(route)
    gate_flat = jnp.concatenate([gate_weights.reshape(-1).astype(jnp.float32), jnp.zeros((1,), jnp.float32)])
    grad_pad = jnp.concatenate([output_gradient, jnp.zeros((1, D), output_gradient.dtype)], axis=0)

    def one_expert(index):
        owner = lax.dynamic_slice_in_dim(holder, index * ROWS, ROWS)
        x_rows = grad_pad[owner // TOPK]
        gate = gate_flat[owner][:, None]
        x_total = jnp.zeros((ROWS, D), jnp.float32)
        g_total = jnp.zeros((ROWS,), jnp.float32)
        for shard in range(SHARDS):
            device_index = index * SHARDS + shard
            upward = jnp.dot(x_rows, w_down[device_index].T, preferred_element_type=jnp.float32)
            pre_gate = lax.dynamic_slice_in_dim(saved_gate, device_index * ROWS, ROWS).astype(jnp.float32)
            pre_up = lax.dynamic_slice_in_dim(saved_up, device_index * ROWS, ROWS).astype(jnp.float32)
            sigma = jax.nn.sigmoid(pre_gate)
            active = pre_gate * sigma
            gate_part = jnp.sum(active * pre_up * upward, axis=1).astype(jnp.bfloat16)
            scaled = gate * upward
            grad_gate_pre = (scaled * pre_up * sigma * (1.0 + pre_gate * (1.0 - sigma))).astype(jnp.bfloat16)
            grad_up_pre = (scaled * active).astype(jnp.bfloat16)
            shard_part = jnp.dot(grad_gate_pre, w_gate[device_index].T, preferred_element_type=jnp.float32)
            shard_part = shard_part + jnp.dot(grad_up_pre, w_up[device_index].T, preferred_element_type=jnp.float32)
            x_total = x_total + shard_part.astype(jnp.bfloat16).astype(jnp.float32)
            g_total = g_total + gate_part.astype(jnp.float32)
        return x_total, g_total

    x_all, g_all = lax.map(one_expert, jnp.arange(EXPERTS, dtype=jnp.int32))
    x_all = x_all.reshape(EXPERTS * ROWS, D)
    g_all = g_all.reshape(EXPERTS * ROWS)
    node_sum = jnp.zeros((tokens * NODES_TOK + 1, D), jnp.float32).at[holder // 2].add(x_all)
    node_sum = node_sum[:-1].astype(jnp.bfloat16).astype(jnp.float32).reshape(tokens, NODES_TOK, D)
    grad_in = jnp.sum(node_sum, axis=1).astype(jnp.bfloat16)
    grad_gate = jnp.zeros((tokens * TOPK + 1,), jnp.bfloat16).at[holder].set(g_all.astype(jnp.bfloat16))
    grad_gate = grad_gate[:-1].reshape(tokens, TOPK)
    return grad_in, grad_gate
```

```python
import jax
import jax.numpy as jnp
from jax import lax
from jax.sharding import PartitionSpec as P

EXP_NODE = 2
TOPK = 8
NODES_TOK = 4
EXTRA = 128


def expert_backward(rows, gate, saved_gate, saved_up, w_gate, w_up, w_down):
    dims = (((1,), (1,)), ((), ()))
    upward = lax.dot_general(rows, w_down, dims, preferred_element_type=jnp.float32)
    pre_gate = saved_gate.astype(jnp.float32)
    pre_up = saved_up.astype(jnp.float32)
    sigma = jax.nn.sigmoid(pre_gate)
    active = pre_gate * sigma
    gate_part = jnp.sum(active * pre_up * upward, axis=1)
    scaled = gate[:, None] * upward
    grad_gate_pre = (scaled * pre_up * sigma * (1.0 + pre_gate * (1.0 - sigma))).astype(
        jnp.bfloat16
    )
    grad_up_pre = (scaled * active).astype(jnp.bfloat16)
    back = lax.dot_general(grad_gate_pre, w_gate, dims, preferred_element_type=jnp.float32)
    back = back + lax.dot_general(grad_up_pre, w_up, dims, preferred_element_type=jnp.float32)
    return back.astype(jnp.bfloat16), gate_part


def exchange(x):
    count, width = x.shape
    x = lax.all_to_all(
        x.reshape(count, 1, width), "node", split_axis=0, concat_axis=0, tiled=True
    )
    return x.reshape(count, width)


def on_device(
    output_gradient, expert_ids, gate_weights, saved_gate, saved_up, w_gate, w_up, w_down
):
    node_count = lax.axis_size("node")
    local_count = lax.axis_size("local")
    tok_count, width = output_gradient.shape
    live_count = tok_count * NODES_TOK
    shard_count = local_count // EXP_NODE
    owner = lax.axis_index("local") // shard_count

    pairs = expert_ids.reshape(tok_count, NODES_TOK, EXP_NODE)
    dest_node = pairs[:, :, 0] // EXP_NODE
    placing = jnp.arange(node_count, dtype=jnp.int32)[:, None, None] == dest_node[None]
    pick = jnp.any(placing, axis=2).astype(jnp.bfloat16)
    hit = (pairs % EXP_NODE)[..., None] == jnp.arange(EXP_NODE, dtype=jnp.int32)
    weights = gate_weights.reshape(tok_count, NODES_TOK, EXP_NODE, 1).astype(jnp.float32)
    route_gate = jnp.sum(jnp.where(hit, weights, 0.0), axis=2)
    send_gate = jnp.sum(jnp.where(placing[..., None], route_gate[None], 0.0), axis=(1, 2))
    send_rows = jnp.dot(pick, output_gradient, preferred_element_type=jnp.float32)
    send = jnp.concatenate(
        [
            send_rows.astype(jnp.bfloat16),
            send_gate.astype(jnp.bfloat16),
            jnp.zeros((node_count, EXTRA - EXP_NODE), jnp.bfloat16),
        ],
        axis=1,
    )
    slots = exchange(send)

    live = (slots[:, width] > 0).astype(jnp.int32)
    rank = jnp.cumsum(live) - live
    compact = (jnp.arange(live_count, dtype=jnp.int32)[:, None] == rank[None]) & (
        live[None] > 0
    )
    compact = compact.astype(jnp.bfloat16)
    rows = jnp.dot(compact, slots, preferred_element_type=jnp.float32).astype(jnp.bfloat16)
    rows = lax.all_gather(rows, "local", axis=0, tiled=True)

    gate = jnp.where(owner == 0, rows[:, width], rows[:, width + 1]).astype(jnp.float32)
    back, gate_part = expert_backward(
        rows[:, :width], gate, saved_gate, saved_up, w_gate[0], w_up[0], w_down[0]
    )
    column = lax.broadcasted_iota(jnp.int32, (back.shape[0], EXTRA), 1)
    extra = jnp.where(column == owner, gate_part[:, None], 0.0).astype(jnp.bfloat16)
    parts = jnp.concatenate([back, extra], axis=1)
    sums = lax.psum_scatter(parts, "local", scatter_dimension=0, tiled=True)

    home = exchange(
        lax.dot_general(
            compact, sums, (((0,), (0,)), ((), ())), preferred_element_type=jnp.float32
        ).astype(jnp.bfloat16)
    )
    grad_in = lax.dot_general(
        pick, home[:, :width], (((0,), (0,)), ((), ())), preferred_element_type=jnp.float32
    ).astype(jnp.bfloat16)
    gates_home = home[:, width : width + EXP_NODE].astype(jnp.float32)
    per_pair = jnp.sum(jnp.where(placing[..., None], gates_home[:, None, None, :], 0.0), axis=0)
    grad_gate = jnp.sum(jnp.where(hit, per_pair[:, :, None, :], 0.0), axis=3)
    return grad_in, grad_gate.reshape(tok_count, TOPK).astype(jnp.bfloat16)


def solution(mesh):
    placed = (
        P(("node", "local"), None),
        P(("node", "local"), None),
        P(("node", "local"), None),
        P(("node", "local"), None),
        P(("node", "local"), None),
        P(("node", "local"), None, None),
        P(("node", "local"), None, None),
        P(("node", "local"), None, None),
    )
    return jax.shard_map(
        on_device,
        mesh=mesh,
        in_specs=placed,
        out_specs=(P(("node", "local"), None), P(("node", "local"), None)),
        check_vma=False,
    )
```

```python
import jax
import jax.numpy as jnp
from jax import lax
from jax.experimental import pallas as pl
from jax.experimental.pallas import tpu as pltpu
from jax.sharding import PartitionSpec as P

EXP_NODE = 2
TOPK = 8
NODES_TOK = 4
EXTRA = 128


def hidden_kernel(owner_ref, up_ref, extra_ref, sgate_ref, sup_ref, wg_ref, wu_ref, out_ref):
    owner = owner_ref[0]
    extra = extra_ref[...]
    column = lax.broadcasted_iota(jnp.int32, extra.shape, 1)
    gate = jnp.sum(jnp.where(column == owner, extra, 0.0), axis=1, keepdims=True)
    shift = jnp.sum(jnp.where(column == EXP_NODE, extra, 0.0), axis=1, keepdims=True)
    upward = up_ref[...] * jnp.exp2(-shift)
    pre_gate = sgate_ref[...].astype(jnp.float32)
    pre_up = sup_ref[...].astype(jnp.float32)
    sigma = jax.nn.sigmoid(pre_gate)
    active = pre_gate * sigma
    gate_part = jnp.sum(active * pre_up * upward, axis=1, keepdims=True)
    scaled = gate * upward
    grad_gate = (scaled * pre_up * sigma * (1.0 + pre_gate * (1.0 - sigma))).astype(jnp.bfloat16)
    grad_up = (scaled * active).astype(jnp.bfloat16)
    dims = (((1,), (1,)), ((), ()))
    width = wg_ref.shape[0]
    step = width // 7 if width % 896 == 0 else width
    for start in range(0, width, step):
        cols = slice(start, start + step)
        back = lax.dot_general(grad_gate, wg_ref[cols, :], dims, preferred_element_type=jnp.float32)
        back += lax.dot_general(grad_up, wu_ref[cols, :], dims, preferred_element_type=jnp.float32)
        out_ref[:, cols] = back.astype(jnp.bfloat16)
    out_ref[:, width:] = jnp.where(column == owner, gate_part, 0.0).astype(jnp.bfloat16)


def hidden_parts(owner, upward, extra, saved_gate, saved_up, w_gate, w_up):
    rows, hidden = upward.shape
    width = w_gate.shape[0]
    block = 128 if rows % 128 == 0 else rows
    by_rows = lambda cols: pl.BlockSpec((block, cols), lambda i: (i, 0))
    whole = lambda shape: pl.BlockSpec(shape, lambda i: (0, 0))
    return pl.pallas_call(
        hidden_kernel,
        grid=(rows // block,),
        in_specs=[
            pl.BlockSpec(memory_space=pltpu.SMEM),
            by_rows(hidden),
            by_rows(EXTRA),
            by_rows(hidden),
            by_rows(hidden),
            whole((width, hidden)),
            whole((width, hidden)),
        ],
        out_specs=by_rows(width + EXTRA),
        out_shape=jax.ShapeDtypeStruct((rows, width + EXTRA), jnp.bfloat16),
        compiler_params=pltpu.CompilerParams(vmem_limit_bytes=24 * 2**20),
        cost_estimate=pl.CostEstimate(
            flops=4 * rows * width * hidden,
            bytes_accessed=4 * width * hidden + 2 * rows * width,
            transcendentals=rows * hidden,
        ),
    )(owner.reshape(1), upward, extra, saved_gate, saved_up, w_gate, w_up)


def power_scale(rows):
    largest = jnp.max(jnp.abs(rows.astype(jnp.float32)), axis=1, keepdims=True)
    scale = jnp.ones_like(largest)
    shift = jnp.zeros_like(largest)
    for bits in (64, 32, 16, 8, 4, 2):
        more = largest * 2.0**bits < 2.0**15
        largest = jnp.where(more, largest * 2.0**bits, largest)
        scale = jnp.where(more, scale * 2.0**bits, scale)
        shift = jnp.where(more, shift + bits, shift)
    return scale, shift


def exchange(x):
    count, width = x.shape
    x = lax.all_to_all(
        x.reshape(count, 1, width), "node", split_axis=0, concat_axis=0, tiled=True
    )
    return x.reshape(count, width)


def on_device(
    output_gradient, expert_ids, gate_weights, saved_gate, saved_up, w_gate, w_up, w_down
):
    node_count = lax.axis_size("node")
    local_count = lax.axis_size("local")
    tok_count, width = output_gradient.shape
    live_count = tok_count * NODES_TOK
    shard_count = local_count // EXP_NODE
    owner = lax.axis_index("local") // shard_count

    pairs = expert_ids.reshape(tok_count, NODES_TOK, EXP_NODE)
    dest_node = pairs[:, :, 0] // EXP_NODE
    placing = jnp.arange(node_count, dtype=jnp.int32)[:, None, None] == dest_node[None]
    pick = jnp.any(placing, axis=2).astype(jnp.bfloat16)
    hit = (pairs % EXP_NODE)[..., None] == jnp.arange(EXP_NODE, dtype=jnp.int32)
    weights = gate_weights.reshape(tok_count, NODES_TOK, EXP_NODE, 1).astype(jnp.float32)
    route_gate = jnp.sum(jnp.where(hit, weights, 0.0), axis=2)
    send_gate = jnp.sum(jnp.where(placing[..., None], route_gate[None], 0.0), axis=(1, 2))
    scale, shift = power_scale(output_gradient)
    scaled = (output_gradient.astype(jnp.float32) * scale).astype(jnp.bfloat16)
    send_rows = jnp.dot(pick, scaled, preferred_element_type=jnp.float32)
    send_shift = jnp.dot(pick, shift.astype(jnp.bfloat16), preferred_element_type=jnp.float32)
    send = jnp.concatenate(
        [
            send_rows.astype(jnp.bfloat16),
            send_gate.astype(jnp.bfloat16),
            send_shift.astype(jnp.bfloat16),
            jnp.zeros((node_count, EXTRA - EXP_NODE - 1), jnp.bfloat16),
        ],
        axis=1,
    )
    slots = exchange(send)

    live = (slots[:, width] > 0).astype(jnp.int32)
    rank = jnp.cumsum(live) - live
    compact = (jnp.arange(live_count, dtype=jnp.int32)[:, None] == rank[None]) & (
        live[None] > 0
    )
    compact = compact.astype(jnp.bfloat16)
    rows = jnp.dot(compact, slots, preferred_element_type=jnp.float32).astype(jnp.float16)
    rows = lax.all_gather(rows, "local", axis=0, tiled=True)

    upward = lax.dot_general(
        rows[:, :width].astype(jnp.bfloat16),
        w_down[0],
        (((1,), (1,)), ((), ())),
        preferred_element_type=jnp.float32,
    )
    extra = rows[:, width:].astype(jnp.float32)
    parts = hidden_parts(
        owner, upward, extra, saved_gate, saved_up, w_gate[0], w_up[0]
    )
    sums = lax.psum_scatter(parts, "local", scatter_dimension=0, tiled=True)

    home = exchange(
        lax.dot_general(
            compact, sums, (((0,), (0,)), ((), ())), preferred_element_type=jnp.float32
        ).astype(jnp.bfloat16)
    )
    grad_in = lax.dot_general(
        pick, home[:, :width], (((0,), (0,)), ((), ())), preferred_element_type=jnp.float32
    ).astype(jnp.bfloat16)
    gates_home = home[:, width : width + EXP_NODE].astype(jnp.float32)
    per_pair = jnp.sum(jnp.where(placing[..., None], gates_home[:, None, None, :], 0.0), axis=0)
    grad_gate = jnp.sum(jnp.where(hit, per_pair[:, :, None, :], 0.0), axis=3)
    return grad_in, grad_gate.reshape(tok_count, TOPK).astype(jnp.bfloat16)


def solution(mesh):
    placed = (
        P(("node", "local"), None),
        P(("node", "local"), None),
        P(("node", "local"), None),
        P(("node", "local"), None),
        P(("node", "local"), None),
        P(("node", "local"), None, None),
        P(("node", "local"), None, None),
        P(("node", "local"), None, None),
    )
    return jax.shard_map(
        on_device,
        mesh=mesh,
        in_specs=placed,
        out_specs=(P(("node", "local"), None), P(("node", "local"), None)),
        check_vma=False,
    )
```

```python
import jax
import jax.numpy as jnp
from jax import lax
from jax.experimental import pallas as pl
from jax.experimental.pallas import tpu as pltpu
from jax.sharding import PartitionSpec as P

EXP_NODE = 2
TOPK = 8
NODES_TOK = 4
EXTRA = 128


def hidden_kernel(where_ref, up_ref, extra_ref, sgate_ref, sup_ref, mine_ref, others_ref):
    owner, parity = where_ref[0], where_ref[1]
    rows, hidden = up_ref.shape
    group = mine_ref.shape[1]
    extra = extra_ref[...]
    column = lax.broadcasted_iota(jnp.int32, extra.shape, 1)
    gate = jnp.sum(jnp.where(column == owner, extra, 0.0), axis=1, keepdims=True)
    shift = jnp.sum(jnp.where(column == EXP_NODE, extra, 0.0), axis=1, keepdims=True)
    upward = up_ref[...] * jnp.exp2(-shift)
    pre_gate = sgate_ref[...].astype(jnp.float32)
    pre_up = sup_ref[...].astype(jnp.float32)
    sigma = jax.nn.sigmoid(pre_gate)
    active = pre_gate * sigma
    gate_part = jnp.sum(active * pre_up * upward, axis=1, keepdims=True)
    scaled = gate * upward
    grad_gate = (scaled * pre_up * sigma * (1.0 + pre_gate * (1.0 - sigma))).astype(jnp.bfloat16)
    grad_up = (scaled * active).astype(jnp.bfloat16)
    terms = jnp.where(column == owner, gate_part, 0.0).astype(jnp.bfloat16)
    for index in range(rows // group):
        here = slice(index * group, (index + 1) * group)
        for keep, ref in ((parity, mine_ref), (1 - parity, others_ref)):

            @pl.when(keep == index % 2)
            def _(ref=ref, here=here, index=index):
                ref[index // 2, :, :hidden] = grad_gate[here]
                ref[index // 2, :, hidden : 2 * hidden] = grad_up[here]
                ref[index // 2, :, 2 * hidden :] = terms[here]


def hidden_grads(where, upward, extra, saved_gate, saved_up, group):
    rows, hidden = upward.shape
    out = jax.ShapeDtypeStruct((rows // group // 2, group, 2 * hidden + EXTRA), jnp.bfloat16)
    return pl.pallas_call(
        hidden_kernel,
        in_specs=[pl.BlockSpec(memory_space=pltpu.SMEM)]
        + [pl.BlockSpec(memory_space=pltpu.VMEM)] * 4,
        out_specs=[pl.BlockSpec(memory_space=pltpu.VMEM)] * 2,
        out_shape=[out, out],
        compiler_params=pltpu.CompilerParams(vmem_limit_bytes=8 * 2**20),
        cost_estimate=pl.CostEstimate(
            flops=20 * rows * hidden, bytes_accessed=8 * rows * hidden, transcendentals=rows * hidden
        ),
    )(where, upward, extra, saved_gate, saved_up)


def parts_kernel(mine_ref, low_h_ref, high_h_ref, own_ref, low_ref, high_ref, out_ref):
    step = pl.program_id(0)
    steps = pl.num_programs(0)
    cols, depth = own_ref.shape
    dims = (((1,), (1,)), ((), ()))

    def times(x, w):
        return lax.dot_general(x, w, dims, preferred_element_type=jnp.float32)

    def write(other_h_ref, other_ref):
        back = times(mine_ref[:, :depth], own_ref[...])
        back += times(other_h_ref[:, :depth], other_ref[...])
        out_ref[:, pl.ds(pl.multiple_of(step * cols, 128), cols)] = back.astype(jnp.bfloat16)

    @pl.when(step < steps // 2)
    def _():
        write(low_h_ref, low_ref)

    @pl.when(step >= steps // 2)
    def _():
        write(high_h_ref, high_ref)

    @pl.when(step == 0)
    def _():
        out_ref[:, out_ref.shape[1] - EXTRA :] = mine_ref[:, depth:] + high_h_ref[:, depth:]


def device_parts(mine, low_h, high_h, own, low, high):
    rows = mine.shape[0]
    width, depth = own.shape
    steps = 4
    cols = width // steps
    whole = lambda x: pl.BlockSpec(x.shape, lambda i: (0, 0))
    return pl.pallas_call(
        parts_kernel,
        grid=(steps,),
        in_specs=[
            whole(mine),
            whole(low_h),
            whole(high_h),
            pl.BlockSpec((cols, depth), lambda i: (i, 0)),
            pl.BlockSpec((cols, depth), lambda i: (jnp.minimum(i, steps // 2 - 1), 0)),
            pl.BlockSpec((cols, depth), lambda i: (jnp.maximum(i - steps // 2, 0), 0)),
        ],
        out_specs=pl.BlockSpec((rows, width + EXTRA), lambda i: (0, 0)),
        out_shape=jax.ShapeDtypeStruct((rows, width + EXTRA), jnp.bfloat16),
        compiler_params=pltpu.CompilerParams(vmem_limit_bytes=24 * 2**20),
        cost_estimate=pl.CostEstimate(
            flops=4 * rows * width * depth,
            bytes_accessed=4 * width * depth + 2 * rows * width,
            transcendentals=0,
        ),
    )(mine, low_h, high_h, own, low, high)


def ring_sum(parts, count, stride, place):
    size = count * stride
    right = [(i, (i + stride) % size) for i in range(size)]
    left = [(i, (i - stride) % size) for i in range(size)]
    rows = parts.shape[0] // count
    cut = (parts.shape[1] // 256) * 128

    def block(offset):
        start = lax.rem(place + offset + count, count) * rows
        return lax.dynamic_slice_in_dim(parts, start, rows)

    def add(x, y):
        return (x.astype(jnp.float32) + y.astype(jnp.float32)).astype(jnp.bfloat16)

    half = count // 2
    far = block(half)
    one = lax.ppermute(far[:, :cut], "local", right)
    two = lax.ppermute(far[:, cut:], "local", left)
    for offset in range(half - 1, 0, -1):
        here, there = block(offset), block(-offset)
        one, two = lax.optimization_barrier((one, two))
        if offset == half - 1:
            one = jnp.concatenate([add(here[:, :cut], one), here[:, cut:]], axis=1)
            two = jnp.concatenate([there[:, :cut], add(there[:, cut:], two)], axis=1)
        else:
            one, two = add(here, one), add(there, two)
        one = lax.ppermute(one, "local", right)
        two = lax.ppermute(two, "local", left)
    own = block(0).astype(jnp.float32)
    if half == 1:
        both = jnp.concatenate([one, two], axis=1).astype(jnp.float32)
    else:
        both = one.astype(jnp.float32) + two.astype(jnp.float32)
    return (own + both).astype(jnp.bfloat16)


def power_scale(rows):
    largest = jnp.max(jnp.abs(rows.astype(jnp.float32)), axis=1, keepdims=True)
    scale = jnp.ones_like(largest)
    shift = jnp.zeros_like(largest)
    for bits in (64, 32, 16, 8, 4, 2):
        more = largest * 2.0**bits < 2.0**15
        largest = jnp.where(more, largest * 2.0**bits, largest)
        scale = jnp.where(more, scale * 2.0**bits, scale)
        shift = jnp.where(more, shift + bits, shift)
    return scale, shift


def exchange(x):
    return lax.all_to_all(x, "node", split_axis=0, concat_axis=0, tiled=True)


def on_device(
    output_gradient, expert_ids, gate_weights, saved_gate, saved_up, w_gate, w_up, w_down
):
    node_count = lax.axis_size("node")
    local_count = lax.axis_size("local")
    tok_count, width = output_gradient.shape
    live_count = tok_count * NODES_TOK
    shard_count = local_count // EXP_NODE

    pairs = expert_ids.reshape(tok_count, NODES_TOK, EXP_NODE)
    dest_node = pairs[:, :, 0] // EXP_NODE
    placing = jnp.arange(node_count, dtype=jnp.int32)[:, None, None] == dest_node[None]
    pick = jnp.any(placing, axis=2).astype(jnp.bfloat16)
    hit = (pairs % EXP_NODE)[..., None] == jnp.arange(EXP_NODE, dtype=jnp.int32)
    weights = gate_weights.reshape(tok_count, NODES_TOK, EXP_NODE, 1).astype(jnp.float32)
    route_gate = jnp.sum(jnp.where(hit, weights, 0.0), axis=2)
    send_gate = jnp.sum(jnp.where(placing[..., None], route_gate[None], 0.0), axis=(1, 2))
    scale, shift = power_scale(output_gradient)
    scaled = (output_gradient.astype(jnp.float32) * scale).astype(jnp.bfloat16)
    send_rows = jnp.dot(pick, scaled, preferred_element_type=jnp.float32)
    send_shift = jnp.dot(pick, shift.astype(jnp.bfloat16), preferred_element_type=jnp.float32)
    send = jnp.concatenate(
        [
            send_rows.astype(jnp.bfloat16),
            send_gate.astype(jnp.bfloat16),
            send_shift.astype(jnp.bfloat16),
            jnp.zeros((node_count, 2 * EXTRA - EXP_NODE - 1), jnp.bfloat16),
        ],
        axis=1,
    ).reshape(node_count, 2, -1)

    place = lax.axis_index("local")
    parity = lax.rem(place, 2)
    half = width // 2
    low_pairs = [(i, i ^ 1) for i in range(local_count)]
    high_pairs = [(i, (i + 2 * (i % 2) - 1) % local_count) for i in range(local_count)]
    own = jnp.concatenate([w_gate[0], w_up[0]], axis=1)
    send, own = lax.optimization_barrier((send, own))
    slots = exchange(send).reshape(node_count, -1)
    low = lax.ppermute(own[:half], "local", low_pairs)
    high = lax.ppermute(own[half:], "local", high_pairs)

    live = (slots[:, width] > 0).astype(jnp.int32)
    rank = jnp.cumsum(live) - live
    compact = (jnp.arange(live_count, dtype=jnp.int32)[:, None] == rank[None]) & (
        live[None] > 0
    )
    compact = compact.astype(jnp.bfloat16)
    rows = jnp.dot(compact, slots, preferred_element_type=jnp.float32)
    rows = rows[:, : width + EXTRA].astype(jnp.float16)
    rows = lax.all_gather(rows, "local", axis=0, tiled=True)

    upward = lax.dot_general(
        rows[:, :width].astype(jnp.bfloat16),
        w_down[0],
        (((1,), (1,)), ((), ())),
        preferred_element_type=jnp.float32,
    )
    mine, others = hidden_grads(
        jnp.stack([place // shard_count, parity]),
        upward,
        rows[:, width:].astype(jnp.float32),
        saved_gate,
        saved_up,
        live_count,
    )
    low_h = lax.ppermute(others, "local", low_pairs)
    high_h = lax.ppermute(others, "local", high_pairs)
    flat = lambda x: x.reshape(-1, x.shape[-1])
    parts = device_parts(flat(mine), flat(low_h), flat(high_h), own, low, high)
    sums = ring_sum(parts, local_count // 2, 2, place // 2)

    back = lax.dot_general(
        compact, sums, (((0,), (0,)), ((), ())), preferred_element_type=jnp.float32
    ).astype(jnp.bfloat16)
    back = jnp.pad(back, ((0, 0), (0, EXTRA))).reshape(node_count, 2, -1)
    home = exchange(back).reshape(node_count, -1)
    grad_in = lax.dot_general(
        pick, home[:, :width], (((0,), (0,)), ((), ())), preferred_element_type=jnp.float32
    ).astype(jnp.bfloat16)
    gates_home = home[:, width : width + EXP_NODE].astype(jnp.float32)
    per_pair = jnp.sum(jnp.where(placing[..., None], gates_home[:, None, None, :], 0.0), axis=0)
    grad_gate = jnp.sum(jnp.where(hit, per_pair[:, :, None, :], 0.0), axis=3)
    return grad_in, grad_gate.reshape(tok_count, TOPK).astype(jnp.bfloat16)


def solution(mesh):
    placed = (
        P(("node", "local"), None),
        P(("node", "local"), None),
        P(("node", "local"), None),
        P(("node", "local"), None),
        P(("node", "local"), None),
        P(("node", "local"), None, None),
        P(("node", "local"), None, None),
        P(("node", "local"), None, None),
    )
    return jax.shard_map(
        on_device,
        mesh=mesh,
        in_specs=placed,
        out_specs=(P(("node", "local"), None), P(("node", "local"), None)),
        check_vma=False,
    )
```

```python
import jax
import jax.numpy as jnp
from jax import lax
from jax.experimental import pallas as pl
from jax.experimental.pallas import tpu as pltpu
from jax.sharding import PartitionSpec as P

EXP_NODE = 2
TOPK = 8
NODES_TOK = 4
EXTRA = 128


def parts_kernel(
    owner_ref,
    extra_ref,
    rows_ref,
    down_own_ref,
    down_low_ref,
    down_high_ref,
    saved_own_ref,
    saved_low_ref,
    saved_high_ref,
    own_gate_ref,
    own_up_ref,
    low_ref,
    high_ref,
    out_ref,
    grads_ref,
):
    step = pl.program_id(0)
    steps = pl.num_programs(0) - 1
    cols, hidden = own_gate_ref.shape
    dims = (((1,), (1,)), ((), ()))

    def times(x, w):
        return lax.dot_general(x, w, dims, preferred_element_type=jnp.float32)

    @pl.when(step == 0)
    def _():
        extra = extra_ref[...]
        column = lax.broadcasted_iota(jnp.int32, extra.shape, 1)

        def pick_column(index):
            return jnp.sum(jnp.where(column == index, extra, 0.0), axis=1, keepdims=True)

        undo = jnp.exp2(-pick_column(EXP_NODE))
        rows = rows_ref[...]
        shards = (
            (down_own_ref, saved_own_ref),
            (down_low_ref, saved_low_ref),
            (down_high_ref, saved_high_ref),
        )
        terms = jnp.zeros(extra.shape, jnp.float32)
        for index, (down_ref, saved_ref) in enumerate(shards):
            owner = owner_ref[index]
            upward = times(rows, down_ref[...]) * undo
            pre_gate = saved_ref[:, :hidden].astype(jnp.float32)
            pre_up = saved_ref[:, hidden:].astype(jnp.float32)
            sigma = jax.nn.sigmoid(pre_gate)
            active = pre_gate * sigma
            scaled = pick_column(owner) * upward
            grad_gate = scaled * pre_up * sigma * (1.0 + pre_gate * (1.0 - sigma))
            grads_ref[index, :, :hidden] = grad_gate.astype(jnp.bfloat16)
            grads_ref[index, :, hidden:] = (scaled * active).astype(jnp.bfloat16)
            if index != 1:
                gate_part = jnp.sum(active * pre_up * upward, axis=1, keepdims=True)
                terms += jnp.where(column == owner, gate_part, 0.0)
        out_ref[:, out_ref.shape[1] - EXTRA :] = terms.astype(jnp.bfloat16)

    def write(index, other_ref):
        back = times(grads_ref[index], other_ref[...])
        back += times(grads_ref[0, :, :hidden], own_gate_ref[...])
        back += times(grads_ref[0, :, hidden:], own_up_ref[...])
        start = pl.multiple_of((step - 1) * cols, 128)
        out_ref[:, pl.ds(start, cols)] = back.astype(jnp.bfloat16)

    @pl.when((step > 0) & (step <= steps // 2))
    def _():
        write(1, low_ref)

    @pl.when(step > steps // 2)
    def _():
        write(2, high_ref)


def device_parts(owners, extra, rows, downs, saved_own, w_gate, w_up, low, high):
    count, depth = saved_own.shape
    width, hidden = w_gate.shape
    steps = 4
    half, cols = width // 2, width // steps
    whole = lambda x: pl.BlockSpec(x.shape, lambda i: (0, 0))
    tail = pl.BlockSpec((count, depth), lambda i: (half // count, 0))
    return pl.pallas_call(
        parts_kernel,
        grid=(steps + 1,),
        in_specs=[pl.BlockSpec(memory_space=pltpu.SMEM), whole(extra), whole(rows)]
        + [whole(x) for x in downs]
        + [whole(saved_own), tail, tail]
        + [
            pl.BlockSpec((cols, hidden), lambda i: (jnp.maximum(i - 1, 0), 0)),
            pl.BlockSpec((cols, hidden), lambda i: (jnp.maximum(i - 1, 0), 0)),
            pl.BlockSpec((cols, depth), lambda i: (jnp.clip(i - 1, 0, steps // 2 - 1), 0)),
            pl.BlockSpec((cols, depth), lambda i: (jnp.maximum(i - 1 - steps // 2, 0), 0)),
        ],
        out_specs=pl.BlockSpec((count, width + EXTRA), lambda i: (0, 0)),
        out_shape=jax.ShapeDtypeStruct((count, width + EXTRA), jnp.bfloat16),
        scratch_shapes=[pltpu.VMEM((3, count, depth), jnp.bfloat16)],
        compiler_params=pltpu.CompilerParams(vmem_limit_bytes=32 * 2**20),
        cost_estimate=pl.CostEstimate(
            flops=14 * count * width * hidden,
            bytes_accessed=14 * width * hidden + 4 * count * width,
            transcendentals=3 * count * hidden,
        ),
    )(owners, extra, rows, *downs, saved_own, low, high, w_gate, w_up, low, high)


def ring_sum(parts, count, stride, place):
    size = count * stride
    right = [(i, (i + stride) % size) for i in range(size)]
    left = [(i, (i - stride) % size) for i in range(size)]
    rows = parts.shape[0] // count
    cut = (parts.shape[1] // 256) * 128

    def block(offset):
        start = lax.rem(place + offset + count, count) * rows
        return lax.dynamic_slice_in_dim(parts, start, rows)

    def add(x, y):
        return (x.astype(jnp.float32) + y.astype(jnp.float32)).astype(jnp.bfloat16)

    half = count // 2
    far = block(half)
    one = lax.ppermute(far[:, :cut], "local", right)
    two = lax.ppermute(far[:, cut:], "local", left)
    for offset in range(half - 1, 0, -1):
        here, there = block(offset), block(-offset)
        one, two = lax.optimization_barrier((one, two))
        if offset == half - 1:
            one = jnp.concatenate([add(here[:, :cut], one), here[:, cut:]], axis=1)
            two = jnp.concatenate([there[:, :cut], add(there[:, cut:], two)], axis=1)
        else:
            one, two = add(here, one), add(there, two)
        one = lax.ppermute(one, "local", right)
        two = lax.ppermute(two, "local", left)
    own = block(0).astype(jnp.float32)
    if half == 1:
        both = jnp.concatenate([one, two], axis=1).astype(jnp.float32)
    else:
        both = one.astype(jnp.float32) + two.astype(jnp.float32)
    return (own + both).astype(jnp.bfloat16)


def power_scale(rows):
    largest = jnp.max(jnp.abs(rows.astype(jnp.float32)), axis=1, keepdims=True)
    scale = jnp.ones_like(largest)
    shift = jnp.zeros_like(largest)
    for bits in (64, 32, 16, 8, 4, 2):
        more = largest * 2.0**bits < 2.0**15
        largest = jnp.where(more, largest * 2.0**bits, largest)
        scale = jnp.where(more, scale * 2.0**bits, scale)
        shift = jnp.where(more, shift + bits, shift)
    return scale, shift


def exchange(x):
    return lax.all_to_all(x, "node", split_axis=0, concat_axis=0, tiled=True)


def on_device(
    output_gradient, expert_ids, gate_weights, saved_gate, saved_up, w_gate, w_up, w_down
):
    node_count = lax.axis_size("node")
    local_count = lax.axis_size("local")
    tok_count, width = output_gradient.shape
    live_count = tok_count * NODES_TOK
    shard_count = local_count // EXP_NODE

    pairs = expert_ids.reshape(tok_count, NODES_TOK, EXP_NODE)
    dest_node = pairs[:, :, 0] // EXP_NODE
    placing = jnp.arange(node_count, dtype=jnp.int32)[:, None, None] == dest_node[None]
    pick = jnp.any(placing, axis=2).astype(jnp.bfloat16)
    hit = (pairs % EXP_NODE)[..., None] == jnp.arange(EXP_NODE, dtype=jnp.int32)
    weights = gate_weights.reshape(tok_count, NODES_TOK, EXP_NODE, 1).astype(jnp.float32)
    route_gate = jnp.sum(jnp.where(hit, weights, 0.0), axis=2)
    send_gate = jnp.sum(jnp.where(placing[..., None], route_gate[None], 0.0), axis=(1, 2))
    scale, shift = power_scale(output_gradient)
    scaled = (output_gradient.astype(jnp.float32) * scale).astype(jnp.bfloat16)
    send_rows = jnp.dot(pick, scaled, preferred_element_type=jnp.float32)
    send_shift = jnp.dot(pick, shift.astype(jnp.bfloat16), preferred_element_type=jnp.float32)
    send = jnp.concatenate(
        [
            send_rows.astype(jnp.bfloat16),
            send_gate.astype(jnp.bfloat16),
            send_shift.astype(jnp.bfloat16),
            jnp.zeros((node_count, 2 * EXTRA - EXP_NODE - 1), jnp.bfloat16),
        ],
        axis=1,
    ).reshape(node_count, 2, -1)

    place = lax.axis_index("local")
    parity = lax.rem(place, 2)
    half = width // 2
    low_pairs = [(i, i ^ 1) for i in range(local_count)]
    high_pairs = [(i, (i + 2 * (i % 2) - 1) % local_count) for i in range(local_count)]
    down = w_down[0]
    down_low = lax.ppermute(down, "local", low_pairs)
    down_high = lax.ppermute(down, "local", high_pairs)
    saved = jnp.concatenate([saved_gate, saved_up], axis=1)
    saved = saved.reshape(local_count // 2, 2, live_count, -1)
    mine, others = (
        lax.dynamic_index_in_dim(saved, which, axis=1, keepdims=False).reshape(
            local_count // 2 * live_count, -1
        )
        for which in (parity, 1 - parity)
    )
    own = jnp.concatenate([w_gate[0], w_up[0]], axis=1)
    low, high = jnp.concatenate([own[:half], others]), jnp.concatenate([own[half:], others])
    send, low, high = lax.optimization_barrier((send, low, high))
    slots = exchange(send).reshape(node_count, -1)
    low = lax.ppermute(low, "local", low_pairs)
    high = lax.ppermute(high, "local", high_pairs)

    live = (slots[:, width] > 0).astype(jnp.int32)
    rank = jnp.cumsum(live) - live
    compact = (jnp.arange(live_count, dtype=jnp.int32)[:, None] == rank[None]) & (
        live[None] > 0
    )
    compact = compact.astype(jnp.bfloat16)
    rows = jnp.dot(compact, slots, preferred_element_type=jnp.float32)
    rows = rows[:, : width + EXTRA].astype(jnp.float16)
    rows = lax.all_gather(
        rows,
        "local",
        axis=0,
        tiled=True,
        axis_index_groups=[list(range(i, local_count, 2)) for i in range(2)],
    )

    step = 2 * parity - 1
    shards = jnp.stack([place, place - step, lax.rem(place + step + local_count, local_count)])
    parts = device_parts(
        shards // shard_count,
        rows[:, width:].astype(jnp.float32),
        rows[:, :width].astype(jnp.bfloat16),
        [down, down_low, down_high],
        mine,
        w_gate[0],
        w_up[0],
        low,
        high,
    )
    sums = ring_sum(parts, local_count // 2, 2, place // 2)

    back = lax.dot_general(
        compact, sums, (((0,), (0,)), ((), ())), preferred_element_type=jnp.float32
    ).astype(jnp.bfloat16)
    back = jnp.pad(back, ((0, 0), (0, EXTRA))).reshape(node_count, 2, -1)
    home = exchange(back).reshape(node_count, -1)
    grad_in = lax.dot_general(
        pick, home[:, :width], (((0,), (0,)), ((), ())), preferred_element_type=jnp.float32
    ).astype(jnp.bfloat16)
    gates_home = home[:, width : width + EXP_NODE].astype(jnp.float32)
    per_pair = jnp.sum(jnp.where(placing[..., None], gates_home[:, None, None, :], 0.0), axis=0)
    grad_gate = jnp.sum(jnp.where(hit, per_pair[:, :, None, :], 0.0), axis=3)
    return grad_in, grad_gate.reshape(tok_count, TOPK).astype(jnp.bfloat16)


def solution(mesh):
    placed = (
        P(("node", "local"), None),
        P(("node", "local"), None),
        P(("node", "local"), None),
        P(("node", "local"), None),
        P(("node", "local"), None),
        P(("node", "local"), None, None),
        P(("node", "local"), None, None),
        P(("node", "local"), None, None),
    )
    return jax.shard_map(
        on_device,
        mesh=mesh,
        in_specs=placed,
        out_specs=(P(("node", "local"), None), P(("node", "local"), None)),
        check_vma=False,
    )
```

```python
import jax
import jax.numpy as jnp
from jax import lax
from jax.experimental import pallas as pl
from jax.experimental.pallas import tpu as pltpu
from jax.sharding import PartitionSpec as P

EXP_NODE = 2
TOPK = 8
NODES_TOK = 4
EXTRA = 128


def parts_kernel(
    owner_ref,
    extra_ref,
    rows_ref,
    down_own_ref,
    down_low_ref,
    down_high_ref,
    saved_own_ref,
    saved_low_ref,
    saved_high_ref,
    own_gate_ref,
    own_up_ref,
    low_ref,
    high_ref,
    out_ref,
    grads_ref,
):
    step = pl.program_id(0)
    steps = pl.num_programs(0) - 1
    cols, hidden = own_gate_ref.shape
    dims = (((1,), (1,)), ((), ()))

    def times(x, w):
        return lax.dot_general(x, w, dims, preferred_element_type=jnp.float32)

    @pl.when(step == 0)
    def _():
        extra = extra_ref[...]
        column = lax.broadcasted_iota(jnp.int32, extra.shape, 1)

        def pick_column(index):
            return jnp.sum(jnp.where(column == index, extra, 0.0), axis=1, keepdims=True)

        undo = jnp.exp2(-pick_column(EXP_NODE))
        rows = rows_ref[...]
        shards = (
            (down_own_ref, saved_own_ref),
            (down_low_ref, saved_low_ref),
            (down_high_ref, saved_high_ref),
        )
        terms = jnp.zeros(extra.shape, jnp.float32)
        for index, (down_ref, saved_ref) in enumerate(shards):
            owner = owner_ref[index]
            upward = times(rows, down_ref[...]) * undo
            pre_gate = saved_ref[:, :hidden].astype(jnp.float32)
            pre_up = saved_ref[:, hidden:].astype(jnp.float32)
            sigma = jax.nn.sigmoid(pre_gate)
            active = pre_gate * sigma
            scaled = pick_column(owner) * upward
            grad_gate = scaled * pre_up * sigma * (1.0 + pre_gate * (1.0 - sigma))
            grads_ref[index, :, :hidden] = grad_gate.astype(jnp.bfloat16)
            grads_ref[index, :, hidden:] = (scaled * active).astype(jnp.bfloat16)
            if index != 1:
                gate_part = jnp.sum(active * pre_up * upward, axis=1, keepdims=True)
                terms += jnp.where(column == owner, gate_part, 0.0)
        out_ref[:, out_ref.shape[1] - EXTRA :] = terms.astype(jnp.bfloat16)

    def write(index, other_ref):
        back = times(grads_ref[index], other_ref[...])
        back += times(grads_ref[0, :, :hidden], own_gate_ref[...])
        back += times(grads_ref[0, :, hidden:], own_up_ref[...])
        start = pl.multiple_of((step - 1) * cols, 128)
        out_ref[:, pl.ds(start, cols)] = back.astype(jnp.bfloat16)

    @pl.when((step > 0) & (step <= steps // 2))
    def _():
        write(1, low_ref)

    @pl.when(step > steps // 2)
    def _():
        write(2, high_ref)


def device_parts(owners, extra, rows, downs, saved_own, w_gate, w_up, low, high):
    count, depth = saved_own.shape
    width, hidden = w_gate.shape
    steps = 4
    half, cols = width // 2, width // steps
    whole = lambda x: pl.BlockSpec(x.shape, lambda i: (0, 0))
    tail = pl.BlockSpec((count, depth), lambda i: (half // count, 0))
    return pl.pallas_call(
        parts_kernel,
        grid=(steps + 1,),
        in_specs=[pl.BlockSpec(memory_space=pltpu.SMEM), whole(extra), whole(rows)]
        + [whole(x) for x in downs]
        + [whole(saved_own), tail, tail]
        + [
            pl.BlockSpec((cols, hidden), lambda i: (jnp.maximum(i - 1, 0), 0)),
            pl.BlockSpec((cols, hidden), lambda i: (jnp.maximum(i - 1, 0), 0)),
            pl.BlockSpec((cols, depth), lambda i: (jnp.clip(i - 1, 0, steps // 2 - 1), 0)),
            pl.BlockSpec((cols, depth), lambda i: (jnp.maximum(i - 1 - steps // 2, 0), 0)),
        ],
        out_specs=pl.BlockSpec((count, width + EXTRA), lambda i: (0, 0)),
        out_shape=jax.ShapeDtypeStruct((count, width + EXTRA), jnp.bfloat16),
        scratch_shapes=[pltpu.VMEM((3, count, depth), jnp.bfloat16)],
        compiler_params=pltpu.CompilerParams(vmem_limit_bytes=32 * 2**20),
        cost_estimate=pl.CostEstimate(
            flops=14 * count * width * hidden,
            bytes_accessed=14 * width * hidden + 4 * count * width,
            transcendentals=3 * count * hidden,
        ),
    )(owners, extra, rows, *downs, saved_own, low, high, w_gate, w_up, low, high)


def ring_sum(parts, count, stride, place):
    size = count * stride
    right = [(i, (i + stride) % size) for i in range(size)]
    left = [(i, (i - stride) % size) for i in range(size)]
    rows = parts.shape[0] // count
    cut = (parts.shape[1] // 256) * 128

    def block(offset):
        start = lax.rem(place + offset + count, count) * rows
        return lax.dynamic_slice_in_dim(parts, start, rows)

    def add(x, y):
        return (x.astype(jnp.float32) + y.astype(jnp.float32)).astype(jnp.bfloat16)

    half = count // 2
    far = block(half)
    one = lax.ppermute(far[:, :cut], "local", right)
    two = lax.ppermute(far[:, cut:], "local", left)
    for offset in range(half - 1, 0, -1):
        here, there = block(offset), block(-offset)
        one, two = lax.optimization_barrier((one, two))
        if offset == half - 1:
            one = jnp.concatenate([add(here[:, :cut], one), here[:, cut:]], axis=1)
            two = jnp.concatenate([there[:, :cut], add(there[:, cut:], two)], axis=1)
        else:
            one, two = add(here, one), add(there, two)
        one = lax.ppermute(one, "local", right)
        two = lax.ppermute(two, "local", left)
    own = block(0).astype(jnp.float32)
    if half == 1:
        both = jnp.concatenate([one, two], axis=1).astype(jnp.float32)
    else:
        both = one.astype(jnp.float32) + two.astype(jnp.float32)
    return (own + both).astype(jnp.bfloat16)


def power_scale(rows):
    largest = jnp.max(jnp.abs(rows.astype(jnp.float32)), axis=1, keepdims=True)
    scale = jnp.ones_like(largest)
    shift = jnp.zeros_like(largest)
    for bits in (64, 32, 16, 8, 4, 2):
        more = largest * 2.0**bits < 2.0**15
        largest = jnp.where(more, largest * 2.0**bits, largest)
        scale = jnp.where(more, scale * 2.0**bits, scale)
        shift = jnp.where(more, shift + bits, shift)
    return scale, shift


def send_kernel(rows_ref, ids_ref, weights_ref, out_ref, table_ref):
    tokens, width = rows_ref.shape
    groups = out_ref.shape[0]
    rows = rows_ref[...]
    scale, shift = power_scale(rows)
    table_ref[:, :width] = jnp.concatenate([rows.astype(jnp.float32) * scale] * NODES_TOK, axis=0)
    column = lax.broadcasted_iota(jnp.int32, (tokens, out_ref.shape[1] - width), 1)
    group = lax.broadcasted_iota(jnp.int32, (tokens, groups), 1)
    weights = weights_ref[...].astype(jnp.float32)
    places = []
    for pair in range(NODES_TOK):
        one, two = 2 * pair, 2 * pair + 1
        name = ids_ref[:, one : one + 1]
        places.append(jnp.where(group == name // EXP_NODE, 1.0, 0.0))
        even = name % EXP_NODE == 0
        first, second = weights[:, one : one + 1], weights[:, two : two + 1]
        table_ref[pair * tokens : (pair + 1) * tokens, width:] = (
            jnp.where(column == 0, jnp.where(even, first, second), 0.0)
            + jnp.where(column == 1, jnp.where(even, second, first), 0.0)
            + jnp.where(column == EXP_NODE, shift, 0.0)
        )
    placed = jnp.concatenate(places, axis=0).astype(jnp.bfloat16)
    out_ref[...] = lax.dot_general(
        placed,
        table_ref[...].astype(jnp.bfloat16),
        (((0,), (0,)), ((), ())),
        preferred_element_type=jnp.float32,
    ).astype(jnp.bfloat16)


def send_slots(rows, ids, weights, groups):
    tokens, width = rows.shape
    total = width + 2 * EXTRA
    return pl.pallas_call(
        send_kernel,
        grid=(1,),
        out_shape=jax.ShapeDtypeStruct((groups, total), jnp.bfloat16),
        in_specs=[pl.BlockSpec(x.shape, lambda i: (0, 0)) for x in (rows, ids, weights)],
        out_specs=pl.BlockSpec((groups, total), lambda i: (0, 0)),
        scratch_shapes=[pltpu.VMEM((tokens * NODES_TOK, total), jnp.float32)],
        compiler_params=pltpu.CompilerParams(vmem_limit_bytes=8 * 2**20),
    )(rows, ids, weights)


def compact_kernel(slots_ref, rows_ref, place_ref):
    count, width = rows_ref.shape
    slots = slots_ref.shape[0]
    live = slots_ref[:, width - EXTRA : width - EXTRA + 1].astype(jnp.float32) > 0
    live = jnp.where(live, 1.0, 0.0)
    row = lax.broadcasted_iota(jnp.int32, (slots, slots), 0)
    column = lax.broadcasted_iota(jnp.int32, (slots, slots), 1)
    ahead = jnp.where(column < row, 1.0, 0.0).astype(jnp.bfloat16)
    spread = jnp.broadcast_to(live, (slots, 128)).astype(jnp.bfloat16)
    rank = jnp.dot(ahead, spread, preferred_element_type=jnp.float32)[:, :1]
    index = lax.broadcasted_iota(jnp.int32, (slots, count), 1).astype(jnp.float32)
    place = jnp.where((index == rank) & (live > 0), 1.0, 0.0).astype(jnp.bfloat16)
    place_ref[...] = place
    rows_ref[...] = lax.dot_general(
        place, slots_ref[:, :width], (((0,), (0,)), ((), ())), preferred_element_type=jnp.float32
    ).astype(jnp.bfloat16)


def compact_slots(slots, count):
    total, width = slots.shape
    return pl.pallas_call(
        compact_kernel,
        out_shape=(
            jax.ShapeDtypeStruct((count, width - EXTRA), jnp.bfloat16),
            jax.ShapeDtypeStruct((total, count), jnp.bfloat16),
        ),
        in_specs=[pl.BlockSpec(memory_space=pltpu.VMEM)],
        out_specs=[pl.BlockSpec(memory_space=pltpu.VMEM)] * 2,
        compiler_params=pltpu.CompilerParams(vmem_limit_bytes=8 * 2**20),
    )(slots)


def exchange(x):
    return lax.all_to_all(x, "node", split_axis=0, concat_axis=0, tiled=True)


def on_device(
    output_gradient, expert_ids, gate_weights, saved_gate, saved_up, w_gate, w_up, w_down
):
    node_count = lax.axis_size("node")
    local_count = lax.axis_size("local")
    tok_count, width = output_gradient.shape
    live_count = tok_count * NODES_TOK
    shard_count = local_count // EXP_NODE

    pairs = expert_ids.reshape(tok_count, NODES_TOK, EXP_NODE)
    dest_node = pairs[:, :, 0] // EXP_NODE
    placing = jnp.arange(node_count, dtype=jnp.int32)[:, None, None] == dest_node[None]
    pick = jnp.any(placing, axis=2).astype(jnp.bfloat16)
    hit = (pairs % EXP_NODE)[..., None] == jnp.arange(EXP_NODE, dtype=jnp.int32)
    send = send_slots(output_gradient, expert_ids, gate_weights, node_count)
    send = send.reshape(node_count, 2, -1)

    place = lax.axis_index("local")
    parity = lax.rem(place, 2)
    half = width // 2
    low_pairs = [(i, i ^ 1) for i in range(local_count)]
    high_pairs = [(i, (i + 2 * (i % 2) - 1) % local_count) for i in range(local_count)]
    down = w_down[0]
    down_low = lax.ppermute(down, "local", low_pairs)
    down_high = lax.ppermute(down, "local", high_pairs)
    send, w_gate, w_up, saved_gate, saved_up = lax.optimization_barrier(
        (send, w_gate, w_up, saved_gate, saved_up)
    )
    saved = jnp.concatenate([saved_gate, saved_up], axis=1)
    saved = saved.reshape(local_count // 2, 2, live_count, -1)
    mine, others = (
        lax.dynamic_index_in_dim(saved, which, axis=1, keepdims=False).reshape(
            local_count // 2 * live_count, -1
        )
        for which in (parity, 1 - parity)
    )
    own = jnp.concatenate([w_gate[0], w_up[0]], axis=1)
    low, high = jnp.concatenate([own[:half], others]), jnp.concatenate([own[half:], others])
    slots = exchange(send).reshape(node_count, -1)
    low = lax.ppermute(low, "local", low_pairs)
    high = lax.ppermute(high, "local", high_pairs)

    rows, compact = compact_slots(slots, live_count)
    rows = rows.astype(jnp.float16)
    rows = lax.all_gather(
        rows,
        "local",
        axis=0,
        tiled=True,
        axis_index_groups=[list(range(i, local_count, 2)) for i in range(2)],
    )

    step = 2 * parity - 1
    shards = jnp.stack([place, place - step, lax.rem(place + step + local_count, local_count)])
    parts = device_parts(
        shards // shard_count,
        rows[:, width:].astype(jnp.float32),
        rows[:, :width].astype(jnp.bfloat16),
        [down, down_low, down_high],
        mine,
        w_gate[0],
        w_up[0],
        low,
        high,
    )
    sums = ring_sum(parts, local_count // 2, 2, place // 2)

    back = lax.dot_general(
        compact, sums, (((1,), (0,)), ((), ())), preferred_element_type=jnp.float32
    ).astype(jnp.bfloat16)
    back = jnp.pad(back, ((0, 0), (0, EXTRA))).reshape(node_count, 2, -1)
    home = exchange(back).reshape(node_count, -1)
    grad_in = lax.dot_general(
        pick, home[:, :width], (((0,), (0,)), ((), ())), preferred_element_type=jnp.float32
    ).astype(jnp.bfloat16)
    gates_home = home[:, width : width + EXP_NODE].astype(jnp.float32)
    per_pair = jnp.sum(jnp.where(placing[..., None], gates_home[:, None, None, :], 0.0), axis=0)
    grad_gate = jnp.sum(jnp.where(hit, per_pair[:, :, None, :], 0.0), axis=3)
    return grad_in, grad_gate.reshape(tok_count, TOPK).astype(jnp.bfloat16)


def solution(mesh):
    placed = (
        P(("node", "local"), None),
        P(("node", "local"), None),
        P(("node", "local"), None),
        P(("node", "local"), None),
        P(("node", "local"), None),
        P(("node", "local"), None, None),
        P(("node", "local"), None, None),
        P(("node", "local"), None, None),
    )
    return jax.shard_map(
        on_device,
        mesh=mesh,
        in_specs=placed,
        out_specs=(P(("node", "local"), None), P(("node", "local"), None)),
        check_vma=False,
    )
```

```python
import jax
import jax.numpy as jnp
from jax import lax
from jax.experimental import pallas as pl
from jax.experimental.pallas import tpu as pltpu
from jax.sharding import PartitionSpec as P

EXP_NODE = 2
TOPK = 8
NODES_TOK = 4
EXTRA = 128


def hidden_kernel(where_ref, up_ref, extra_ref, sgate_ref, sup_ref, mine_ref, others_ref):
    owner, parity = where_ref[0], where_ref[1]
    rows, hidden = up_ref.shape
    group = mine_ref.shape[1]
    extra = extra_ref[...]
    column = lax.broadcasted_iota(jnp.int32, extra.shape, 1)
    gate = jnp.sum(jnp.where(column == owner, extra, 0.0), axis=1, keepdims=True)
    shift = jnp.sum(jnp.where(column == EXP_NODE, extra, 0.0), axis=1, keepdims=True)
    upward = up_ref[...] * jnp.exp2(-shift)
    pre_gate = sgate_ref[...].astype(jnp.float32)
    pre_up = sup_ref[...].astype(jnp.float32)
    sigma = jax.nn.sigmoid(pre_gate)
    active = pre_gate * sigma
    gate_part = jnp.sum(active * pre_up * upward, axis=1, keepdims=True)
    scaled = gate * upward
    grad_gate = (scaled * pre_up * sigma * (1.0 + pre_gate * (1.0 - sigma))).astype(jnp.bfloat16)
    grad_up = (scaled * active).astype(jnp.bfloat16)
    terms = jnp.where(column == owner, gate_part, 0.0).astype(jnp.bfloat16)
    for index in range(rows // group):
        here = slice(index * group, (index + 1) * group)
        for keep, ref in ((parity, mine_ref), (1 - parity, others_ref)):

            @pl.when(keep == index % 2)
            def _(ref=ref, here=here, index=index):
                ref[index // 2, :, :hidden] = grad_gate[here]
                ref[index // 2, :, hidden : 2 * hidden] = grad_up[here]
                ref[index // 2, :, 2 * hidden :] = terms[here]


def hidden_grads(where, upward, extra, saved_gate, saved_up, group):
    rows, hidden = upward.shape
    out = jax.ShapeDtypeStruct((rows // group // 2, group, 2 * hidden + EXTRA), jnp.bfloat16)
    return pl.pallas_call(
        hidden_kernel,
        in_specs=[pl.BlockSpec(memory_space=pltpu.SMEM)]
        + [pl.BlockSpec(memory_space=pltpu.VMEM)] * 4,
        out_specs=[pl.BlockSpec(memory_space=pltpu.VMEM)] * 2,
        out_shape=[out, out],
        compiler_params=pltpu.CompilerParams(vmem_limit_bytes=8 * 2**20),
        cost_estimate=pl.CostEstimate(
            flops=20 * rows * hidden, bytes_accessed=8 * rows * hidden, transcendentals=rows * hidden
        ),
    )(where, upward, extra, saved_gate, saved_up)


def parts_kernel(mine_ref, low_h_ref, high_h_ref, own_ref, low_ref, high_ref, out_ref):
    step = pl.program_id(0)
    steps = pl.num_programs(0)
    cols, depth = own_ref.shape
    dims = (((1,), (1,)), ((), ()))

    def times(x, w):
        return lax.dot_general(x, w, dims, preferred_element_type=jnp.float32)

    def write(other_h_ref, other_ref):
        back = times(mine_ref[:, :depth], own_ref[...])
        back += times(other_h_ref[:, :depth], other_ref[...])
        out_ref[:, pl.ds(pl.multiple_of(step * cols, 128), cols)] = back.astype(jnp.bfloat16)

    @pl.when(step < steps // 2)
    def _():
        write(low_h_ref, low_ref)

    @pl.when(step >= steps // 2)
    def _():
        write(high_h_ref, high_ref)

    @pl.when(step == 0)
    def _():
        out_ref[:, out_ref.shape[1] - EXTRA :] = mine_ref[:, depth:] + high_h_ref[:, depth:]


def device_parts(mine, low_h, high_h, own, low, high):
    rows = mine.shape[0]
    width, depth = own.shape
    steps = 4
    cols = width // steps
    whole = lambda x: pl.BlockSpec(x.shape, lambda i: (0, 0))
    return pl.pallas_call(
        parts_kernel,
        grid=(steps,),
        in_specs=[
            whole(mine),
            whole(low_h),
            whole(high_h),
            pl.BlockSpec((cols, depth), lambda i: (i, 0)),
            pl.BlockSpec((cols, depth), lambda i: (jnp.minimum(i, steps // 2 - 1), 0)),
            pl.BlockSpec((cols, depth), lambda i: (jnp.maximum(i - steps // 2, 0), 0)),
        ],
        out_specs=pl.BlockSpec((rows, width + EXTRA), lambda i: (0, 0)),
        out_shape=jax.ShapeDtypeStruct((rows, width + EXTRA), jnp.bfloat16),
        compiler_params=pltpu.CompilerParams(vmem_limit_bytes=24 * 2**20),
        cost_estimate=pl.CostEstimate(
            flops=4 * rows * width * depth,
            bytes_accessed=4 * width * depth + 2 * rows * width,
            transcendentals=0,
        ),
    )(mine, low_h, high_h, own, low, high)


def ring_sum(parts, count, stride, place):
    size = count * stride
    right = [(i, (i + stride) % size) for i in range(size)]
    left = [(i, (i - stride) % size) for i in range(size)]
    rows = parts.shape[0] // count
    cut = (parts.shape[1] // 256) * 128

    def block(offset):
        start = lax.rem(place + offset + count, count) * rows
        return lax.dynamic_slice_in_dim(parts, start, rows)

    def add(x, y):
        return (x.astype(jnp.float32) + y.astype(jnp.float32)).astype(jnp.bfloat16)

    half = count // 2
    far = block(half)
    one = lax.ppermute(far[:, :cut], "local", right)
    two = lax.ppermute(far[:, cut:], "local", left)
    for offset in range(half - 1, 0, -1):
        here, there = block(offset), block(-offset)
        one, two = lax.optimization_barrier((one, two))
        if offset == half - 1:
            one = jnp.concatenate([add(here[:, :cut], one), here[:, cut:]], axis=1)
            two = jnp.concatenate([there[:, :cut], add(there[:, cut:], two)], axis=1)
        else:
            one, two = add(here, one), add(there, two)
        one = lax.ppermute(one, "local", right)
        two = lax.ppermute(two, "local", left)
    own = block(0).astype(jnp.float32)
    if half == 1:
        both = jnp.concatenate([one, two], axis=1).astype(jnp.float32)
    else:
        both = one.astype(jnp.float32) + two.astype(jnp.float32)
    return (own + both).astype(jnp.bfloat16)


def power_scale(rows):
    largest = jnp.max(jnp.abs(rows.astype(jnp.float32)), axis=1, keepdims=True)
    scale = jnp.ones_like(largest)
    shift = jnp.zeros_like(largest)
    for bits in (64, 32, 16, 8, 4, 2):
        more = largest * 2.0**bits < 2.0**15
        largest = jnp.where(more, largest * 2.0**bits, largest)
        scale = jnp.where(more, scale * 2.0**bits, scale)
        shift = jnp.where(more, shift + bits, shift)
    return scale, shift


def send_kernel(rows_ref, ids_ref, weights_ref, out_ref, table_ref):
    tokens, width = rows_ref.shape
    groups = out_ref.shape[0]
    rows = rows_ref[...]
    scale, shift = power_scale(rows)
    table_ref[:, :width] = jnp.concatenate([rows.astype(jnp.float32) * scale] * NODES_TOK, axis=0)
    column = lax.broadcasted_iota(jnp.int32, (tokens, out_ref.shape[1] - width), 1)
    group = lax.broadcasted_iota(jnp.int32, (tokens, groups), 1)
    weights = weights_ref[...].astype(jnp.float32)
    places = []
    for pair in range(NODES_TOK):
        one, two = 2 * pair, 2 * pair + 1
        name = ids_ref[:, one : one + 1]
        places.append(jnp.where(group == name // EXP_NODE, 1.0, 0.0))
        even = name % EXP_NODE == 0
        first, second = weights[:, one : one + 1], weights[:, two : two + 1]
        table_ref[pair * tokens : (pair + 1) * tokens, width:] = (
            jnp.where(column == 0, jnp.where(even, first, second), 0.0)
            + jnp.where(column == 1, jnp.where(even, second, first), 0.0)
            + jnp.where(column == EXP_NODE, shift, 0.0)
        )
    placed = jnp.concatenate(places, axis=0).astype(jnp.bfloat16)
    out_ref[...] = lax.dot_general(
        placed,
        table_ref[...].astype(jnp.bfloat16),
        (((0,), (0,)), ((), ())),
        preferred_element_type=jnp.float32,
    ).astype(jnp.bfloat16)


def send_slots(rows, ids, weights, groups):
    tokens, width = rows.shape
    total = width + 2 * EXTRA
    return pl.pallas_call(
        send_kernel,
        grid=(1,),
        out_shape=jax.ShapeDtypeStruct((groups, total), jnp.bfloat16),
        in_specs=[pl.BlockSpec(x.shape, lambda i: (0, 0)) for x in (rows, ids, weights)],
        out_specs=pl.BlockSpec((groups, total), lambda i: (0, 0)),
        scratch_shapes=[pltpu.VMEM((tokens * NODES_TOK, total), jnp.float32)],
        compiler_params=pltpu.CompilerParams(vmem_limit_bytes=8 * 2**20),
    )(rows, ids, weights)


def compact_kernel(slots_ref, rows_ref, place_ref):
    count, width = rows_ref.shape
    slots = slots_ref.shape[0]
    live = slots_ref[:, width - EXTRA : width - EXTRA + 1].astype(jnp.float32) > 0
    live = jnp.where(live, 1.0, 0.0)
    row = lax.broadcasted_iota(jnp.int32, (slots, slots), 0)
    column = lax.broadcasted_iota(jnp.int32, (slots, slots), 1)
    ahead = jnp.where(column < row, 1.0, 0.0).astype(jnp.bfloat16)
    spread = jnp.broadcast_to(live, (slots, 128)).astype(jnp.bfloat16)
    rank = jnp.dot(ahead, spread, preferred_element_type=jnp.float32)[:, :1]
    index = lax.broadcasted_iota(jnp.int32, (slots, count), 1).astype(jnp.float32)
    place = jnp.where((index == rank) & (live > 0), 1.0, 0.0).astype(jnp.bfloat16)
    place_ref[...] = place
    rows_ref[...] = lax.dot_general(
        place, slots_ref[:, :width], (((0,), (0,)), ((), ())), preferred_element_type=jnp.float32
    ).astype(jnp.bfloat16)


def compact_slots(slots, count):
    total, width = slots.shape
    return pl.pallas_call(
        compact_kernel,
        out_shape=(
            jax.ShapeDtypeStruct((count, width - EXTRA), jnp.bfloat16),
            jax.ShapeDtypeStruct((total, count), jnp.bfloat16),
        ),
        in_specs=[pl.BlockSpec(memory_space=pltpu.VMEM)],
        out_specs=[pl.BlockSpec(memory_space=pltpu.VMEM)] * 2,
        compiler_params=pltpu.CompilerParams(vmem_limit_bytes=8 * 2**20),
    )(slots)


def exchange(x):
    return lax.all_to_all(x, "node", split_axis=0, concat_axis=0, tiled=True)


def on_device(
    output_gradient, expert_ids, gate_weights, saved_gate, saved_up, w_gate, w_up, w_down
):
    node_count = lax.axis_size("node")
    local_count = lax.axis_size("local")
    tok_count, width = output_gradient.shape
    live_count = tok_count * NODES_TOK
    shard_count = local_count // EXP_NODE

    pairs = expert_ids.reshape(tok_count, NODES_TOK, EXP_NODE)
    dest_node = pairs[:, :, 0] // EXP_NODE
    placing = jnp.arange(node_count, dtype=jnp.int32)[:, None, None] == dest_node[None]
    pick = jnp.any(placing, axis=2).astype(jnp.bfloat16)
    hit = (pairs % EXP_NODE)[..., None] == jnp.arange(EXP_NODE, dtype=jnp.int32)
    send = send_slots(output_gradient, expert_ids, gate_weights, node_count)
    send = send.reshape(node_count, 2, -1)

    place = lax.axis_index("local")
    parity = lax.rem(place, 2)
    half = width // 2
    low_pairs = [(i, i ^ 1) for i in range(local_count)]
    high_pairs = [(i, (i + 2 * (i % 2) - 1) % local_count) for i in range(local_count)]
    own = jnp.concatenate([w_gate[0], w_up[0]], axis=1)
    send, own = lax.optimization_barrier((send, own))
    slots = exchange(send).reshape(node_count, -1)
    low = lax.ppermute(own[:half], "local", low_pairs)
    high = lax.ppermute(own[half:], "local", high_pairs)

    rows, compact = compact_slots(slots, live_count)
    rows = rows.astype(jnp.float16)
    rows = lax.all_gather(rows, "local", axis=0, tiled=True)

    upward = lax.dot_general(
        rows[:, :width].astype(jnp.bfloat16),
        w_down[0],
        (((1,), (1,)), ((), ())),
        preferred_element_type=jnp.float32,
    )
    mine, others = hidden_grads(
        jnp.stack([place // shard_count, parity]),
        upward,
        rows[:, width:].astype(jnp.float32),
        saved_gate,
        saved_up,
        live_count,
    )
    low_h = lax.ppermute(others, "local", low_pairs)
    high_h = lax.ppermute(others, "local", high_pairs)
    flat = lambda x: x.reshape(-1, x.shape[-1])
    parts = device_parts(flat(mine), flat(low_h), flat(high_h), own, low, high)
    sums = ring_sum(parts, local_count // 2, 2, place // 2)

    back = lax.dot_general(
        compact, sums, (((1,), (0,)), ((), ())), preferred_element_type=jnp.float32
    ).astype(jnp.bfloat16)
    back = jnp.pad(back, ((0, 0), (0, EXTRA))).reshape(node_count, 2, -1)
    home = exchange(back).reshape(node_count, -1)
    grad_in = lax.dot_general(
        pick, home[:, :width], (((0,), (0,)), ((), ())), preferred_element_type=jnp.float32
    ).astype(jnp.bfloat16)
    gates_home = home[:, width : width + EXP_NODE].astype(jnp.float32)
    per_pair = jnp.sum(jnp.where(placing[..., None], gates_home[:, None, None, :], 0.0), axis=0)
    grad_gate = jnp.sum(jnp.where(hit, per_pair[:, :, None, :], 0.0), axis=3)
    return grad_in, grad_gate.reshape(tok_count, TOPK).astype(jnp.bfloat16)


def solution(mesh):
    placed = (
        P(("node", "local"), None),
        P(("node", "local"), None),
        P(("node", "local"), None),
        P(("node", "local"), None),
        P(("node", "local"), None),
        P(("node", "local"), None, None),
        P(("node", "local"), None, None),
        P(("node", "local"), None, None),
    )
    return jax.shard_map(
        on_device,
        mesh=mesh,
        in_specs=placed,
        out_specs=(P(("node", "local"), None), P(("node", "local"), None)),
        check_vma=False,
    )
```
